32 devices in a mesh: parts: 2 (over x), leaf: 16 (over z, y, core).
Axes of the slice: x: 2, y: 2, z: 4, core: 2. Of those that a mesh axis runs over, the one named last changes fastest.
Arguments:
- krylov: float32 [8, 131072], P(None, ('parts', 'leaf')), parts along dimension 1, may hold values from -6 to 6
- tree_perm: int32 [131072], P(('parts', 'leaf')), parts along dimension 0, may hold values from 0 to 4095, as said below
- owner: int32 [512], P('parts'), parts along dimension 0, may hold values from 0 to 255, as said below
- near_src: int32 [1024], P(('parts', 'leaf')), parts along dimension 0, may hold values from -1 to 255, as said below
- near_tgt: int32 [1024], P(('parts', 'leaf')), parts along dimension 0, may hold values from 0 to 15
- near_blocks: float32 [1024, 256, 256], P(('parts', 'leaf')), parts along dimension 0, may hold values from -0.375 to 0.375
- basis: float32 [32, 131072], P(None, ('parts', 'leaf')), parts along dimension 1, may hold values from -0.375 to 0.375
- transfer: float32 [32, 16384], P(None, ('parts', 'leaf')), parts along dimension 1, may hold values from -0.25 to 0.25
- top_coup: float32 [1024, 512], P(('parts', 'leaf')), parts along dimension 0, may hold values from -0.25 to 0.25
- far_src: int32 [2048], P(('parts', 'leaf')), parts along dimension 0, may hold values from 0 to 255
- far_coup: float32 [32, 65536], P(None, ('parts', 'leaf')), parts along dimension 1, may hold values from -0.5 to 0.5
Outputs:
- next_vector: float32 [131072], P(('parts', 'leaf')), parts along dimension 0
- coeffs: float32 [18], P('parts'), parts along dimension 0
The draws below stay inside these ranges and needn't reach their ends.
There are 2 independent parts, one for each index of `parts`. The reference program is written for one: setup_inputs(seed, part) draws one part's arguments, and reference() takes and returns one part's arrays. A program takes and returns all parts, laid end to end along the dimension named above; each array names one. Nothing has to cross between parts.
Inputs may be any that keep to these rules, and one draw needn't show every extreme that they name: `tree_perm`: each device's block of 4096 entries is a permutation of 0 to 4095. `owner`: A permutation of 0 to 255. `near_src`: on device d, slots g * 8 to (g + 1) * 8 - 1 name leaves stored (by owner) on device (d + s_g) mod 16, with s = (0, -1, 1, -2) for g = 0, 1, 2, 3. Live slots of a device come first, at least 8 of them; some device has all 32 live.
All inputs are finite; a program needn't handle non-finite values.
Results may differ from the reference program's by a relative error of at most 0.000061.
Values sent between devices are 32-bit elements; how exact they have to be, the bound alone decides.
A program may use at most 64 MiB of HBM per device.

```python
import jax
import jax.numpy as jnp
from jax import lax

M = 256
K = 32
LB = 16
CAP = 8
NNEAR = 32
NF = 4
J = 8
LOC = 4096
NL = 256
NTOT = 65536
N_LEAF = 16


def owner_table(key):
    return jax.random.permutation(jax.random.fold_in(key, 11), NL).astype(jnp.int32)


def draw_owner(key, part):
    return owner_table(key)


def draw_tree_perm(key, part):
    key = jax.random.fold_in(key, 7)
    keys = jax.random.split(key, N_LEAF)
    table = jax.vmap(lambda k: jax.random.permutation(k, LB * M))(keys)
    return table.reshape(-1).astype(jnp.int32)


def draw_near_src(key, part):
    owners = owner_table(key)
    inverse = jnp.argsort(owners, stable=True).astype(jnp.int32)
    key = jax.random.fold_in(key, 5)
    key_loc, key_cnt, key_full = jax.random.split(key, 3)
    steps_tab = jnp.array([0, -1, 1, -2], dtype=jnp.int32)
    devices = jnp.arange(N_LEAF, dtype=jnp.int32)
    source_dev = (devices[:, None] + steps_tab[None, :] + N_LEAF) % N_LEAF
    source_dev = jnp.repeat(source_dev, CAP, axis=1)
    local = jax.random.randint(key_loc, (N_LEAF, NNEAR), 0, LB, dtype=jnp.int32)
    counts = jax.random.randint(key_cnt, (N_LEAF,), CAP, NNEAR + 1, dtype=jnp.int32)
    full = jax.random.randint(key_full, (), 0, N_LEAF, dtype=jnp.int32)
    counts = jnp.where(devices == full, NNEAR, counts)
    live = jnp.arange(NNEAR, dtype=jnp.int32)[None, :] < counts[:, None]
    cluster = inverse[source_dev * LB + local]
    return jnp.where(live, cluster, -1).reshape(-1).astype(jnp.int32)


def with_ends(entries, rng, least, high):
    longest = entries.shape.index(max(entries.shape))
    spots = []
    for shift in (0, 1):
        where = [jax.random.randint(jax.random.fold_in(rng, axis), (), 0, length) for axis, length in enumerate(entries.shape)]
        where[longest] = (where[longest] + shift) % entries.shape[longest]
        spots.append(tuple(where))
    return entries.at[spots[0]].set(least).at[spots[1]].set(high)


def block_scale(rng, shape, cuts, low, top_value):
    gain, own = 1.0, jax.random.fold_in(rng, 6)
    for axis_at, parts in cuts:
        steps = jnp.exp(jax.random.uniform(jax.random.fold_in(own, axis_at), (parts,), jnp.float32, low / len(cuts), top_value / len(cuts)))
        gain = gain * jnp.repeat(steps, shape[axis_at] // parts).reshape([-1 if axis == axis_at else 1 for axis in range(len(shape))])
    return gain


def bell_draw(rng, dims, scale, bound, pieces=(), kind=jnp.bfloat16):
    values = scale * jax.random.normal(rng, dims, jnp.float32)
    if pieces:
        values = values * block_scale(rng, dims, pieces, -0.22, 0.18)
    return jnp.clip(values, -bound, bound).astype(kind)


def setup_inputs(seed: int = 0, part: int = 0) -> dict:
    seeds = jax.random.split(jax.random.key(seed), 12)
    part_keys = jax.random.split(jax.random.fold_in(seeds[11], part), 12)
    krylov = bell_draw(part_keys[0], (J, NTOT), 1.0, 6.0, ((1, 16),), jnp.float32)
    tree_perm = draw_tree_perm(jax.random.fold_in(jax.random.fold_in(seeds[11], part), 71), part)
    owner = draw_owner(jax.random.fold_in(jax.random.fold_in(seeds[11], part), 71), part)
    near_src = draw_near_src(jax.random.fold_in(jax.random.fold_in(seeds[11], part), 71), part)
    near_tgt = with_ends(jax.random.randint(part_keys[4], (N_LEAF * NNEAR,), 0, LB), jax.random.fold_in(part_keys[4], 1), 0, LB - 1).astype(jnp.int32)
    near_blocks = bell_draw(part_keys[5], (N_LEAF * NNEAR, M, M), M ** -0.5, 0.375, ((0, 16),), jnp.float32)
    basis = bell_draw(part_keys[6], (K, NTOT), M ** -0.5, 0.375, ((1, 16),), jnp.float32)
    transfer = bell_draw(part_keys[7], (K, NL * K), (LB * K) ** -0.5, 0.25, ((1, 16),), jnp.float32)
    top_coup = bell_draw(part_keys[8], (N_LEAF * K, N_LEAF * K), (N_LEAF * K) ** -0.5, 0.25, ((0, 16),), jnp.float32)
    far_src = with_ends(jax.random.randint(part_keys[9], (NL * NF,), 0, NL), jax.random.fold_in(part_keys[9], 1), 0, NL - 1).astype(jnp.int32)
    far_coup = bell_draw(part_keys[10], (K, NL * NF * K), (NF * K) ** -0.5, 0.5, ((1, 16),), jnp.float32)
    return dict(krylov=krylov, tree_perm=tree_perm, owner=owner, near_src=near_src, near_tgt=near_tgt, near_blocks=near_blocks, basis=basis, transfer=transfer, top_coup=top_coup, far_src=far_src, far_coup=far_coup)


HI = lax.Precision.HIGHEST

def reference(krylov, tree_perm, owner, near_src, near_tgt, near_blocks, basis, transfer, top_coup, far_src, far_coup):
    x = krylov[J - 1]
    perm_rows = tree_perm.reshape(N_LEAF, LOC)
    xc = jnp.take_along_axis(x.reshape(N_LEAF, LOC), perm_rows, axis=1).reshape(NL, M)
    bases = basis.reshape(K, NL, M)
    coef = jnp.einsum('knm,nm->nk', bases, xc, precision=HI)
    trans = transfer.reshape(K, N_LEAF, LB, K)
    parent = jnp.einsum('adcb,dcb->da', trans, coef.reshape(N_LEAF, LB, K), precision=HI)
    keep = 1.0 - jnp.eye(N_LEAF, dtype=jnp.float32)
    top = top_coup.reshape(N_LEAF, K, N_LEAF, K)
    field_top = jnp.einsum('daeb,de,eb->da', top, keep, parent, precision=HI)
    field = jnp.einsum('adcb,da->dcb', trans, field_top, precision=HI).reshape(NL, K)
    far_rows = coef[owner[far_src]].reshape(NL, NF, K)
    field = field + jnp.einsum('acfb,cfb->ca', far_coup.reshape(K, NL, NF, K), far_rows, precision=HI)
    yc = jnp.einsum('knm,nk->nm', bases, field, precision=HI)
    live = near_src >= 0
    slots = owner[jnp.maximum(near_src, 0)]
    src_rows = xc[slots]
    contrib = jnp.einsum('nab,nb->na', near_blocks, src_rows, precision=HI)
    contrib = contrib * live[:, None].astype(jnp.float32)
    target = jnp.arange(N_LEAF * NNEAR, dtype=jnp.int32) // NNEAR * LB + near_tgt
    yc = yc + jax.ops.segment_sum(contrib, target, num_segments=NL)
    rows = jnp.arange(N_LEAF, dtype=jnp.int32)[:, None]
    y = jnp.zeros((N_LEAF, LOC), jnp.float32).at[rows, perm_rows].set(yc.reshape(N_LEAF, LOC)).reshape(NTOT)
    w = 0.5 * x + y
    h = jnp.dot(krylov, w, precision=HI) / NTOT
    wp = w - jnp.dot(h, krylov, precision=HI)
    beta = jnp.sqrt(jnp.sum(wp * wp) / NTOT + 1e-06)
    return (wp / beta, jnp.concatenate([h, beta[None]]))
```

```python
import functools

import jax
import jax.numpy as jnp
from jax import lax
from jax.experimental import pallas as pl
from jax.experimental.pallas import tpu as pltpu
from jax.sharding import PartitionSpec as P

M = 256
K = 32
CAP = 8
NF = 4
J = 8
LANES = 128
MESH = pl.DeviceIdType.MESH
F32 = jnp.float32
BF16 = jnp.bfloat16


def iota(shape, dim):
    return lax.broadcasted_iota(jnp.int32, shape, dim)


def split3(v):
    a = v.astype(BF16)
    r = v - a.astype(F32)
    b = r.astype(BF16)
    c = (r - b.astype(F32)).astype(BF16)
    return a, b, c


def rowsum(v):
    return jnp.sum(v, axis=0, keepdims=True)


def lanesum(v):
    return jnp.sum(v, axis=1, keepdims=True)


def kernel(
    ndev, leaves, total,
    kry_h, perm_h, basis_h, trans_h, top_h, far_h, nb_h,
    owner_s, nsrc_s, ntgt_s, fsrc_s,
    out_ref, coef_ref,
    kry, perm, basis, trans, top, far, nb,
    x32, oh, xown, xin1, xin2, xin3, land1, land2, rolled, idx, ybuf,
    lsem, nsem, xsend, xrecv, s1, r1, s2, r2,
):
    me = lax.axis_index("leaf")
    chunks = leaves * 2
    groups = leaves // 4

    def peer(k):
        return {"leaf": lax.rem(me + k, ndev)}

    def local(i, src, dst):
        return pltpu.make_async_copy(src, dst, lsem.at[i])

    loads = [
        local(i, s, d)
        for i, (s, d) in enumerate(
            ((kry_h, kry), (perm_h, perm), (basis_h, basis), (trans_h, trans), (top_h, top), (far_h, far))
        )
    ]
    near = [
        pltpu.make_async_copy(nb_h.at[pl.ds(g * CAP, CAP)], nb.at[pl.ds(g * CAP, CAP)], nsem.at[g])
        for g in range(4)
    ]
    for cp in loads[:4]:
        cp.start()
    barrier = pltpu.get_barrier_semaphore()

    def greet(k, _):
        pl.semaphore_signal(barrier, inc=1, device_id=peer(k), device_id_type=MESH)
        return 0

    lax.fori_loop(1, ndev, greet, 0)
    for cp in near:
        cp.start()
    for cp in loads[4:]:
        cp.start()

    sub8 = iota((8, LANES), 0)
    lane8 = iota((8, LANES), 1)
    sub32 = iota((K, LANES), 0)
    lane32 = iota((K, LANES), 1)
    lane1 = iota((1, LANES), 1)

    loads[1].wait()
    sub128 = iota((LANES, LANES), 0)
    for i in range(chunks):
        lo = perm[i : i + 1, :] & (LANES - 1)
        oh[:, i * LANES : (i + 1) * LANES] = jnp.where(sub128 == lo, 1.0, 0.0).astype(BF16)
    loads[0].wait()
    for i in range(chunks):
        x32[i : i + 1, :] = kry[J - 1 : J, i * LANES : (i + 1) * LANES]
    x3 = jnp.concatenate(split3(x32[...]), axis=0)
    for i in range(chunks):
        a = jnp.dot(x3, oh[:, i * LANES : (i + 1) * LANES], preferred_element_type=F32)
        a = a[:chunks] + a[chunks : 2 * chunks] + a[2 * chunks :]
        hi = perm[i : i + 1, :] >> 7
        half = (i % 2) * LANES
        xown[i // 2 : i // 2 + 1, half : half + LANES] = rowsum(jnp.where(iota((chunks, LANES), 0) == hi, a, 0.0))

    pl.semaphore_wait(barrier, ndev - 1)

    xbufs = (xown, xin1, xin2, xin3)
    xcopies = [
        pltpu.make_async_remote_copy(
            src_ref=xown,
            dst_ref=xbufs[g],
            send_sem=xsend.at[g],
            recv_sem=xrecv.at[g],
            device_id=peer(hop + ndev),
            device_id_type=MESH,
        )
        for g, hop in ((1, 1), (2, -1), (3, 2))
    ]
    for cp in xcopies:
        cp.start()

    loads[2].wait()
    loads[3].wait()
    tile = jnp.zeros((8, LANES), F32)
    qacc = jnp.zeros((K, LANES), F32)
    for t in range(groups):
        acc = jnp.zeros((K, LANES), F32)
        for cc in range(4):
            c = 4 * t + cc
            p = (
                basis[:, c * M : c * M + LANES] * xown[c : c + 1, :LANES]
                + basis[:, c * M + LANES : (c + 1) * M] * xown[c : c + 1, LANES:]
            )
            acc = acc + jnp.where(lane32 == cc * K + sub32, lanesum(p), 0.0)
        row = rowsum(acc)
        qacc = qacc + trans[:, t * LANES : (t + 1) * LANES] * row
        tile = jnp.where(sub8 == t, row, tile)
    qrow = rowsum(jnp.where(lane32 % K == sub32, lanesum(qacc), 0.0))
    land1[me] = jnp.where(sub8 == groups, qrow, tile)

    def send1(k):
        return pltpu.make_async_remote_copy(
            src_ref=land1.at[me],
            dst_ref=land1.at[me],
            send_sem=s1.at[k],
            recv_sem=r1.at[k],
            device_id=peer(k),
            device_id_type=MESH,
        )

    def recv1(k):
        src = lax.rem(me - k + ndev, ndev)
        return pltpu.make_async_remote_copy(
            src_ref=land1.at[src],
            dst_ref=land1.at[src],
            send_sem=s1.at[k],
            recv_sem=r1.at[k],
            device_id=peer(k),
            device_id_type=MESH,
        )

    def start1(k, _):
        send1(k).start()
        return 0

    lax.fori_loop(1, ndev, start1, 0)

    rows = iota((leaves, M), 0)
    sub16 = iota((16, M), 0)
    yc = jnp.zeros((leaves, M), F32)
    for g in range(4):
        near[g].wait()
        if g:
            xcopies[g - 1].wait_recv()

        def slot(i, yc):
            n = g * CAP + i
            src = nsrc_s[n]
            loc = lax.rem(owner_s[jnp.maximum(src, 0)], leaves)
            x = xbufs[g][pl.ds(loc, 1), :]
            xh = x.astype(BF16).astype(F32)
            lhs = jnp.where(sub16 == 0, xh, jnp.where(sub16 == 1, x - xh, 0.0)).astype(BF16)
            blk = nb[n]
            bh = blk.astype(BF16)
            bl = (blk - bh.astype(F32)).astype(BF16)
            dims = (((1,), (1,)), ((), ()))
            r = lax.dot_general(lhs, bh, dims, preferred_element_type=F32)
            r = r + lax.dot_general(lhs, bl, dims, preferred_element_type=F32)
            tgt = jnp.where(src >= 0, ntgt_s[n], -1)
            return yc + jnp.where(rows == tgt, r[0:1] + r[1:2], 0.0)

        yc = lax.fori_loop(0, CAP, slot, yc, unroll=True)

    gram = jnp.zeros((8, LANES), F32)
    for k in range(J):
        acc = jnp.zeros((8, LANES), F32)
        for i in range(chunks):
            part = kry[:, i * LANES : (i + 1) * LANES]
            acc = acc + part * kry[k : k + 1, i * LANES : (i + 1) * LANES]
        gram = gram + jnp.where(lane8 % J == k, lanesum(acc), 0.0)
    message = jnp.where(lane8 // J == sub8, gram, 0.0)

    stride = ndev * 8
    for i in range(leaves * NF):
        s = owner_s[fsrc_s[i]]
        c = lax.rem(s, leaves)
        turn = (i % NF - c) & 3
        idx[i] = turn * stride + (s // leaves) * 8 + c // 4

    def wait1(k, _):
        recv1(k).wait_recv()
        return 0

    lax.fori_loop(1, ndev, wait1, 0)

    got = land1[...].reshape(stride, LANES)
    rolled[0:stride, :] = got
    for s in range(1, 4):
        rolled[s * stride : (s + 1) * stride, :] = pltpu.roll(got, K * s, 1)
    loads[4].wait()
    loads[5].wait()
    gacc = jnp.zeros((K, LANES), F32)
    for t in range(ndev // 4):
        row = jnp.zeros((1, LANES), F32)
        for ee in range(4):
            e = 4 * t + ee
            row = row + jnp.where((lane1 // K == ee) & (me != e), land1[e, groups : groups + 1, :], 0.0)
        gacc = gacc + top[:, t * LANES : (t + 1) * LANES] * row
    gcol = lanesum(gacc)

    y3 = jnp.zeros((3 * chunks, LANES), F32)
    for c in range(leaves):
        t, cc = c // 4, c % 4
        if cc == 0:
            grow = rowsum(trans[:, t * LANES : (t + 1) * LANES] * gcol)
        r = jnp.zeros((1, LANES), F32)
        for f in range(NF):
            r = jnp.where(lane1 // K == f, rolled[pl.ds(idx[c * NF + f], 1), :], r)
        acc = far[:, c * LANES : (c + 1) * LANES] * r + jnp.where(lane32 == cc * K + sub32, grow, 0.0)
        g = lanesum(acc)
        for half in range(2):
            i = 2 * c + half
            yrow = yc[c : c + 1, half * LANES : (half + 1) * LANES] + rowsum(basis[:, i * LANES : (i + 1) * LANES] * g)
            hit = iota((chunks, LANES), 0) == perm[i : i + 1, :] >> 7
            lhs = jnp.concatenate([jnp.where(hit, v.astype(F32), 0.0).astype(BF16) for v in split3(yrow)], axis=0)
            y3 = y3 + lax.dot_general(
                lhs, oh[:, i * LANES : (i + 1) * LANES], (((1,), (1,)), ((), ())), preferred_element_type=F32
            )
    y = y3[:chunks] + y3[chunks : 2 * chunks] + y3[2 * chunks :]
    ybuf[...] = y

    acc = jnp.zeros((8, LANES), F32)
    sq = jnp.zeros((8, LANES), F32)
    for i in range(chunks):
        acc = acc + kry[:, i * LANES : (i + 1) * LANES] * ybuf[i : i + 1, :]
    for i in range(chunks // 8):
        sq = sq + ybuf[8 * i : 8 * i + 8, :] * ybuf[8 * i : 8 * i + 8, :]
    message = message + jnp.where(lane8 == 64 + sub8, lanesum(acc), 0.0)
    message = message + jnp.where(lane8 == 72, lanesum(sq), 0.0)
    land2[me] = rowsum(message)

    def send2(k):
        return pltpu.make_async_remote_copy(
            src_ref=land2.at[me],
            dst_ref=land2.at[me],
            send_sem=s2.at[k],
            recv_sem=r2.at[k],
            device_id=peer(k),
            device_id_type=MESH,
        )

    def recv2(k):
        src = lax.rem(me - k + ndev, ndev)
        return pltpu.make_async_remote_copy(
            src_ref=land2.at[src],
            dst_ref=land2.at[src],
            send_sem=s2.at[k],
            recv_sem=r2.at[k],
            device_id=peer(k),
            device_id_type=MESH,
        )

    def start2(k, _):
        send2(k).start()
        return 0

    def wait2(k, _):
        recv2(k).wait_recv()
        return 0

    lax.fori_loop(1, ndev, start2, 0)
    for cp in xcopies:
        cp.wait_send()

    def sent1(k, _):
        send1(k).wait_send()
        return 0

    lax.fori_loop(1, ndev, sent1, 0)
    lax.fori_loop(1, ndev, wait2, 0)

    sums = land2[0]
    for e in range(1, ndev):
        sums = sums + land2[e]
    ky = lanesum(jnp.where(lane8 == 64 + sub8, sums, 0.0))
    kx = lanesum(jnp.where(lane8 == (J - 1) * J + sub8, sums, 0.0))
    h = (0.5 * kx + ky) * (1.0 / total)
    is_x = iota((8, 1), 0) == J - 1
    d = h - jnp.where(is_x, 0.5, 0.0)
    left = rowsum(jnp.where(lane8 // J == sub8, d, 0.0))
    right = rowsum(jnp.where(lane8 % J == sub8, d, 0.0))
    along = rowsum(jnp.where(lane8 == 64 + sub8, -2.0 * d, 0.0))
    terms = sums * (left * right + along + jnp.where(lane1 == 72, 1.0, 0.0))
    squares = jnp.maximum(lanesum(terms), 0.0) * (1.0 / total)
    beta = jnp.sqrt(squares + 1e-06)
    coef_ref[...] = (rowsum(jnp.where(lane8 == sub8, h, 0.0)) + jnp.where(lane1 == J, beta, 0.0))[:, : J + 1]
    for i in range(chunks):
        out_ref[i : i + 1, :] = (ybuf[i : i + 1, :] - rowsum(kry[:, i * LANES : (i + 1) * LANES] * d)) / beta

    def sent2(k, _):
        send2(k).wait_send()
        return 0

    lax.fori_loop(1, ndev, sent2, 0)


def on_device(
    krylov,
    tree_perm,
    owner,
    near_src,
    near_tgt,
    near_blocks,
    basis,
    transfer,
    top_coup,
    far_src,
    far_coup,
):
    ndev = lax.axis_size("leaf")
    local_rows = tree_perm.shape[0]
    leaves = local_rows // M
    chunks = local_rows // LANES
    hbm = pl.BlockSpec(memory_space=pl.ANY)
    smem = pl.BlockSpec(memory_space=pltpu.SMEM)
    vmem = pl.BlockSpec(memory_space=pltpu.VMEM)
    arrays = (krylov, tree_perm.reshape(chunks, LANES), basis, transfer, top_coup, far_coup, near_blocks)
    dma = pltpu.SemaphoreType.DMA
    nxt, coeffs = pl.pallas_call(
        functools.partial(kernel, ndev, leaves, float(local_rows * ndev)),
        out_shape=(
            jax.ShapeDtypeStruct((chunks, LANES), F32),
            jax.ShapeDtypeStruct((1, J + 1), F32),
        ),
        in_specs=[hbm] * 7 + [smem] * 4,
        out_specs=(vmem, vmem),
        scratch_shapes=[pltpu.VMEM(a.shape, a.dtype) for a in arrays]
        + [
            pltpu.VMEM((chunks, LANES), F32),
            pltpu.VMEM((LANES, local_rows), BF16),
            pltpu.VMEM((leaves, M), F32),
            pltpu.VMEM((leaves, M), F32),
            pltpu.VMEM((leaves, M), F32),
            pltpu.VMEM((leaves, M), F32),
            pltpu.VMEM((ndev, 8, LANES), F32),
            pltpu.VMEM((ndev, 1, LANES), F32),
            pltpu.VMEM((4 * ndev * 8, LANES), F32),
            pltpu.SMEM((leaves * NF,), jnp.int32),
            pltpu.VMEM((chunks, LANES), F32),
            dma((6,)),
            dma((4,)),
            dma((4,)),
            dma((4,)),
            dma((ndev,)),
            dma((ndev,)),
            dma((ndev,)),
            dma((ndev,)),
        ],
        compiler_params=pltpu.CompilerParams(
            collective_id=0, has_side_effects=True, vmem_limit_bytes=40 * 1024 * 1024
        ),
        cost_estimate=pl.CostEstimate(flops=20_000_000, bytes_accessed=10_000_000, transcendentals=0),
    )(*arrays, owner, near_src, near_tgt, far_src)
    return nxt.reshape(local_rows), coeffs.reshape(J + 1)


def solution(mesh):
    return jax.shard_map(
        on_device,
        mesh=mesh,
        in_specs=(
            P(None, ("parts", "leaf")),
            P(("parts", "leaf")),
            P("parts"),
            P(("parts", "leaf")),
            P(("parts", "leaf")),
            P(("parts", "leaf"), None, None),
            P(None, ("parts", "leaf")),
            P(None, ("parts", "leaf")),
            P(("parts", "leaf"), None),
            P(("parts", "leaf")),
            P(None, ("parts", "leaf")),
        ),
        out_specs=(P(("parts", "leaf")), P("parts")),
        check_vma=False,
    )
```

```python
import functools

import jax
import jax.numpy as jnp
from jax import lax
from jax.experimental import pallas as pl
from jax.experimental.pallas import tpu as pltpu
from jax.sharding import PartitionSpec as P

M = 256
K = 32
CAP = 8
NF = 4
J = 8
LANES = 128
MESH = pl.DeviceIdType.MESH
F32 = jnp.float32
BF16 = jnp.bfloat16


def iota(shape, dim):
    return lax.broadcasted_iota(jnp.int32, shape, dim)


def split3(v):
    a = v.astype(BF16)
    r = v - a.astype(F32)
    b = r.astype(BF16)
    c = (r - b.astype(F32)).astype(BF16)
    return a, b, c


def rowsum(v):
    return jnp.sum(v, axis=0, keepdims=True)


def lanesum(v):
    return jnp.sum(v, axis=1, keepdims=True)


def kernel(
    ndev, leaves, total,
    kry_h, perm_h, basis_h, trans_h, top_h, far_h, nb_h,
    owner_h, nsrc_h, ntgt_h, fsrc_h,
    out_ref,
    kry, perm, basis, trans, top, far, nb, owner_s, nsrc_s, ntgt_s, fsrc_s,
    x32, oh, xown, xin1, xin2, xin3, land1, land2, rolled, idx, ybuf,
    lsem, nsem, xsend, xrecv, s1, r1, s2, r2,
):
    me = lax.axis_index("leaf")
    chunks = leaves * 2
    groups = leaves // 4
    shift = leaves.bit_length() - 1

    def wrap(i):
        return jnp.where(i >= ndev, i - ndev, i)

    def peer(k):
        return {"leaf": wrap(me + k)}

    def local(i, src, dst):
        return pltpu.make_async_copy(src, dst, lsem.at[i])

    loads = [
        local(i, s, d)
        for i, (s, d) in enumerate(
            ((kry_h, kry), (perm_h, perm), (basis_h, basis), (trans_h, trans), (top_h, top), (far_h, far),
             (owner_h, owner_s), (nsrc_h, nsrc_s), (ntgt_h, ntgt_s), (fsrc_h, fsrc_s))
        )
    ]
    near = [
        pltpu.make_async_copy(nb_h.at[pl.ds(g * CAP, CAP)], nb.at[pl.ds(g * CAP, CAP)], nsem.at[g])
        for g in range(4)
    ]
    for cp in loads[:3]:
        cp.start()
    barrier = pltpu.get_barrier_semaphore()

    def greet(k, _):
        pl.semaphore_signal(barrier, inc=1, device_id=peer(k), device_id_type=MESH)
        return 0

    lax.fori_loop(1, ndev, greet, 0)
    for cp in near:
        cp.start()
    for cp in loads[3:]:
        cp.start()

    sub8 = iota((8, LANES), 0)
    lane8 = iota((8, LANES), 1)
    sub32 = iota((K, LANES), 0)
    lane32 = iota((K, LANES), 1)
    lane1 = iota((1, LANES), 1)

    loads[1].wait()
    sub128 = iota((LANES, LANES), 0)
    for i in range(chunks):
        lo = perm[i : i + 1, :] & (LANES - 1)
        oh[:, i * LANES : (i + 1) * LANES] = jnp.where(sub128 == lo, 1.0, 0.0).astype(BF16)
    loads[0].wait()
    for i in range(chunks):
        x32[i : i + 1, :] = kry[J - 1 : J, i * LANES : (i + 1) * LANES]
    x3 = jnp.concatenate(split3(x32[...]), axis=0)
    for i in range(chunks):
        a = jnp.dot(x3, oh[:, i * LANES : (i + 1) * LANES], preferred_element_type=F32)
        a = a[:chunks] + a[chunks : 2 * chunks] + a[2 * chunks :]
        hi = perm[i : i + 1, :] >> 7
        half = (i % 2) * LANES
        xown[i // 2 : i // 2 + 1, half : half + LANES] = rowsum(jnp.where(iota((chunks, LANES), 0) == hi, a, 0.0))

    pl.semaphore_wait(barrier, ndev - 1)

    xbufs = (xown, xin1, xin2, xin3)
    xcopies = [
        pltpu.make_async_remote_copy(
            src_ref=xown,
            dst_ref=xbufs[g],
            send_sem=xsend.at[g],
            recv_sem=xrecv.at[g],
            device_id=peer(hop % ndev),
            device_id_type=MESH,
        )
        for g, hop in ((1, 1), (2, -1), (3, 2))
    ]
    for cp in xcopies:
        cp.start()

    loads[2].wait()
    loads[3].wait()
    tile = jnp.zeros((8, LANES), F32)
    qacc = jnp.zeros((K, LANES), F32)
    for t in range(groups):
        acc = jnp.zeros((K, LANES), F32)
        for cc in range(4):
            c = 4 * t + cc
            p = (
                basis[:, c * M : c * M + LANES] * xown[c : c + 1, :LANES]
                + basis[:, c * M + LANES : (c + 1) * M] * xown[c : c + 1, LANES:]
            )
            acc = acc + jnp.where(lane32 == cc * K + sub32, lanesum(p), 0.0)
        row = rowsum(acc)
        qacc = qacc + trans[:, t * LANES : (t + 1) * LANES] * row
        tile = jnp.where(sub8 == t, row, tile)
    qrow = rowsum(jnp.where((lane32 & (K - 1)) == sub32, lanesum(qacc), 0.0))
    land1[me] = jnp.where(sub8 == groups, qrow, tile)

    def send1(k):
        return pltpu.make_async_remote_copy(
            src_ref=land1.at[me],
            dst_ref=land1.at[me],
            send_sem=s1.at[k],
            recv_sem=r1.at[k],
            device_id=peer(k),
            device_id_type=MESH,
        )

    def recv1(k):
        src = wrap(me - k + ndev)
        return pltpu.make_async_remote_copy(
            src_ref=land1.at[src],
            dst_ref=land1.at[src],
            send_sem=s1.at[k],
            recv_sem=r1.at[k],
            device_id=peer(k),
            device_id_type=MESH,
        )

    def start1(k, _):
        send1(k).start()
        return 0

    lax.fori_loop(1, ndev, start1, 0)

    for cp in loads[6:]:
        cp.wait()
    rows = iota((leaves, M), 0)
    sub16 = iota((16, M), 0)
    yc = jnp.zeros((leaves, M), F32)
    for g in range(4):
        near[g].wait()
        if g:
            xcopies[g - 1].wait_recv()

        def slot(i, yc):
            n = g * CAP + i
            src = nsrc_s[n]
            loc = owner_s[jnp.maximum(src, 0)] & (leaves - 1)
            x = xbufs[g][pl.ds(loc, 1), :]
            xh = x.astype(BF16).astype(F32)
            lhs = jnp.where(sub16 == 0, xh, jnp.where(sub16 == 1, x - xh, 0.0)).astype(BF16)
            blk = nb[n]
            bh = blk.astype(BF16)
            bl = (blk - bh.astype(F32)).astype(BF16)
            dims = (((1,), (1,)), ((), ()))
            r = lax.dot_general(lhs, bh, dims, preferred_element_type=F32)
            r = r + lax.dot_general(lhs, bl, dims, preferred_element_type=F32)
            tgt = jnp.where(src >= 0, ntgt_s[n], -1)
            return yc + jnp.where(rows == tgt, r[0:1] + r[1:2], 0.0)

        yc = lax.fori_loop(0, CAP, slot, yc, unroll=True)

    gram = jnp.zeros((8, LANES), F32)
    for k in range(J):
        acc = jnp.zeros((8, LANES), F32)
        for i in range(chunks):
            part = kry[:, i * LANES : (i + 1) * LANES]
            acc = acc + part * kry[k : k + 1, i * LANES : (i + 1) * LANES]
        gram = gram + jnp.where((lane8 & (J - 1)) == k, lanesum(acc), 0.0)
    message = jnp.where((lane8 >> 3) == sub8, gram, 0.0)

    stride = ndev * 8
    for i in range(leaves * NF):
        s = owner_s[fsrc_s[i]]
        turn = (i % NF - s) & 3
        idx[i] = turn * stride + (s >> shift) * 8 + ((s & (leaves - 1)) >> 2)

    def wait1(k, _):
        recv1(k).wait_recv()
        return 0

    lax.fori_loop(1, ndev, wait1, 0)

    got = land1[...].reshape(stride, LANES)
    rolled[0:stride, :] = got
    for s in range(1, 4):
        rolled[s * stride : (s + 1) * stride, :] = pltpu.roll(got, K * s, 1)
    loads[4].wait()
    loads[5].wait()
    gacc = jnp.zeros((K, LANES), F32)
    for t in range(ndev // 4):
        row = jnp.zeros((1, LANES), F32)
        for ee in range(4):
            e = 4 * t + ee
            row = row + jnp.where(((lane1 >> 5) == ee) & (me != e), land1[e, groups : groups + 1, :], 0.0)
        gacc = gacc + top[:, t * LANES : (t + 1) * LANES] * row
    gcol = lanesum(gacc)

    y3 = jnp.zeros((2 * chunks, LANES), F32)
    for c in range(leaves):
        t, cc = c // 4, c % 4
        if cc == 0:
            grow = rowsum(trans[:, t * LANES : (t + 1) * LANES] * gcol)
        r = jnp.zeros((1, LANES), F32)
        for f in range(NF):
            r = jnp.where((lane1 >> 5) == f, rolled[pl.ds(idx[c * NF + f], 1), :], r)
        acc = far[:, c * LANES : (c + 1) * LANES] * r + jnp.where(lane32 == cc * K + sub32, grow, 0.0)
        g = lanesum(acc)
        yrow = yc[c : c + 1, :] + rowsum(basis[:, c * M : (c + 1) * M] * g)
        hi = jnp.concatenate([perm[2 * c : 2 * c + 1, :], perm[2 * c + 1 : 2 * c + 2, :]], axis=1) >> 7
        hit = iota((chunks, M), 0) == hi
        top_half = yrow.astype(BF16).astype(F32)
        lhs = jnp.concatenate([jnp.where(hit, v, 0.0).astype(BF16) for v in (top_half, yrow - top_half)], axis=0)
        y3 = y3 + lax.dot_general(
            lhs, oh[:, c * M : (c + 1) * M], (((1,), (1,)), ((), ())), preferred_element_type=F32
        )
    y = y3[:chunks] + y3[chunks:]
    ybuf[...] = y

    acc = jnp.zeros((8, LANES), F32)
    sq = jnp.zeros((8, LANES), F32)
    for i in range(chunks):
        acc = acc + kry[:, i * LANES : (i + 1) * LANES] * ybuf[i : i + 1, :]
    for i in range(chunks // 8):
        sq = sq + ybuf[8 * i : 8 * i + 8, :] * ybuf[8 * i : 8 * i + 8, :]
    message = message + jnp.where(lane8 == 64 + sub8, lanesum(acc), 0.0)
    message = message + jnp.where(lane8 == 72, lanesum(sq), 0.0)
    land2[me] = rowsum(message)

    def send2(k):
        return pltpu.make_async_remote_copy(
            src_ref=land2.at[me],
            dst_ref=land2.at[me],
            send_sem=s2.at[k],
            recv_sem=r2.at[k],
            device_id=peer(k),
            device_id_type=MESH,
        )

    def recv2(k):
        src = wrap(me - k + ndev)
        return pltpu.make_async_remote_copy(
            src_ref=land2.at[src],
            dst_ref=land2.at[src],
            send_sem=s2.at[k],
            recv_sem=r2.at[k],
            device_id=peer(k),
            device_id_type=MESH,
        )

    def start2(k, _):
        send2(k).start()
        return 0

    def wait2(k, _):
        recv2(k).wait_recv()
        return 0

    lax.fori_loop(1, ndev, start2, 0)
    for cp in xcopies:
        cp.wait_send()

    def sent1(k, _):
        send1(k).wait_send()
        return 0

    lax.fori_loop(1, ndev, sent1, 0)
    lax.fori_loop(1, ndev, wait2, 0)

    sums = land2[0]
    for e in range(1, ndev):
        sums = sums + land2[e]
    ky = lanesum(jnp.where(lane8 == 64 + sub8, sums, 0.0))
    kx = lanesum(jnp.where(lane8 == (J - 1) * J + sub8, sums, 0.0))
    h = (0.5 * kx + ky) * (1.0 / total)
    is_x = iota((8, 1), 0) == J - 1
    d = h - jnp.where(is_x, 0.5, 0.0)
    left = rowsum(jnp.where((lane8 >> 3) == sub8, d, 0.0))
    right = rowsum(jnp.where((lane8 & (J - 1)) == sub8, d, 0.0))
    along = rowsum(jnp.where(lane8 == 64 + sub8, -2.0 * d, 0.0))
    terms = sums * (left * right + along + jnp.where(lane1 == 72, 1.0, 0.0))
    squares = jnp.maximum(lanesum(terms), 0.0) * (1.0 / total)
    beta = jnp.sqrt(squares + 1e-06)
    coef = rowsum(jnp.where(lane8 == sub8, h, 0.0)) + jnp.where(lane1 == J, beta, 0.0)
    out_ref[chunks:, :] = jnp.where(sub8 == 0, coef, 0.0)
    for i in range(chunks):
        out_ref[i : i + 1, :] = (ybuf[i : i + 1, :] - rowsum(kry[:, i * LANES : (i + 1) * LANES] * d)) / beta

    def sent2(k, _):
        send2(k).wait_send()
        return 0

    lax.fori_loop(1, ndev, sent2, 0)


def take_apart(both_ref, nxt_ref, coef_ref):
    nxt_ref[...] = both_ref[: nxt_ref.shape[0], :]
    coef_ref[...] = both_ref[nxt_ref.shape[0] : nxt_ref.shape[0] + 1, : J + 1]


def on_device(
    krylov,
    tree_perm,
    owner,
    near_src,
    near_tgt,
    near_blocks,
    basis,
    transfer,
    top_coup,
    far_src,
    far_coup,
):
    ndev = lax.axis_size("leaf")
    local_rows = tree_perm.shape[0]
    leaves = local_rows // M
    chunks = local_rows // LANES
    hbm = pl.BlockSpec(memory_space=pltpu.HBM)
    vmem = pl.BlockSpec(memory_space=pltpu.VMEM)
    arrays = (krylov, tree_perm.reshape(chunks, LANES), basis, transfer, top_coup, far_coup, near_blocks)
    indices = (owner, near_src, near_tgt, far_src)
    dma = pltpu.SemaphoreType.DMA
    both = pl.pallas_call(
        functools.partial(kernel, ndev, leaves, float(local_rows * ndev)),
        out_shape=jax.ShapeDtypeStruct((chunks + 8, LANES), F32),
        in_specs=[hbm] * 11,
        out_specs=vmem,
        scratch_shapes=[pltpu.VMEM(a.shape, a.dtype) for a in arrays]
        + [pltpu.SMEM(a.shape, a.dtype) for a in indices]
        + [
            pltpu.VMEM((chunks, LANES), F32),
            pltpu.VMEM((LANES, local_rows), BF16),
            pltpu.VMEM((leaves, M), F32),
            pltpu.VMEM((leaves, M), F32),
            pltpu.VMEM((leaves, M), F32),
            pltpu.VMEM((leaves, M), F32),
            pltpu.VMEM((ndev, 8, LANES), F32),
            pltpu.VMEM((ndev, 1, LANES), F32),
            pltpu.VMEM((4 * ndev * 8, LANES), F32),
            pltpu.SMEM((leaves * NF,), jnp.int32),
            pltpu.VMEM((chunks, LANES), F32),
            dma((10,)),
            dma((4,)),
            dma((4,)),
            dma((4,)),
            dma((ndev,)),
            dma((ndev,)),
            dma((ndev,)),
            dma((ndev,)),
        ],
        compiler_params=pltpu.CompilerParams(
            collective_id=0, has_side_effects=True, vmem_limit_bytes=60 * 1024 * 1024
        ),
        cost_estimate=pl.CostEstimate(flops=20_000_000, bytes_accessed=10_000_000, transcendentals=0),
    )(*arrays, *indices)
    nxt, coeffs = pl.pallas_call(
        take_apart,
        out_shape=(
            jax.ShapeDtypeStruct((chunks, LANES), F32),
            jax.ShapeDtypeStruct((1, J + 1), F32),
        ),
        in_specs=[vmem],
        out_specs=(vmem, vmem),
    )(both)
    return nxt.reshape(local_rows), coeffs.reshape(J + 1)


def solution(mesh):
    return jax.shard_map(
        on_device,
        mesh=mesh,
        in_specs=(
            P(None, ("parts", "leaf")),
            P(("parts", "leaf")),
            P("parts"),
            P(("parts", "leaf")),
            P(("parts", "leaf")),
            P(("parts", "leaf"), None, None),
            P(None, ("parts", "leaf")),
            P(None, ("parts", "leaf")),
            P(("parts", "leaf"), None),
            P(("parts", "leaf")),
            P(None, ("parts", "leaf")),
        ),
        out_specs=(P(("parts", "leaf")), P("parts")),
        check_vma=False,
    )
```

```python
import functools

import jax
import jax.numpy as jnp
from jax import lax
from jax.experimental import pallas as pl
from jax.experimental.pallas import tpu as pltpu
from jax.sharding import PartitionSpec as P

M = 256
K = 32
CAP = 8
NF = 4
J = 8
LANES = 128
MESH = pl.DeviceIdType.MESH
F32 = jnp.float32
BF16 = jnp.bfloat16


def iota(shape, dim):
    return lax.broadcasted_iota(jnp.int32, shape, dim)


def split3(v):
    a = v.astype(BF16)
    r = v - a.astype(F32)
    b = r.astype(BF16)
    c = (r - b.astype(F32)).astype(BF16)
    return a, b, c


def rowsum(v):
    return jnp.sum(v, axis=0, keepdims=True)


def lanesum(v):
    return jnp.sum(v, axis=1, keepdims=True)


def kernel(
    ndev, leaves, total,
    kry_h, perm_h, basis_h, trans_h, top_h, far_h, nb_h,
    owner_h, nsrc_h, ntgt_h, fsrc_h,
    out_ref,
    kry, perm, basis, trans, top, far, nb, owner_s, nsrc_s, ntgt_s, fsrc_s,
    x32, oh, xown, xin1, xin2, xin3, land1, land2, rolled, idx, ybuf,
    lsem, nsem, xsend, xrecv, s1, r1, s2, r2,
):
    me = lax.axis_index("leaf")
    chunks = leaves * 2
    groups = leaves // 4
    shift = leaves.bit_length() - 1

    def wrap(i):
        return jnp.where(i >= ndev, i - ndev, i)

    def peer(k):
        return {"leaf": wrap(me + k)}

    def local(i, src, dst):
        return pltpu.make_async_copy(src, dst, lsem.at[i])

    loads = [
        local(i, s, d)
        for i, (s, d) in enumerate(
            ((kry_h, kry), (perm_h, perm), (basis_h, basis), (trans_h, trans), (top_h, top), (far_h, far),
             (owner_h, owner_s), (nsrc_h, nsrc_s), (ntgt_h, ntgt_s), (fsrc_h, fsrc_s))
        )
    ]
    near = [
        pltpu.make_async_copy(nb_h.at[pl.ds(g * CAP, CAP)], nb.at[pl.ds(g * CAP, CAP)], nsem.at[g])
        for g in range(4)
    ]
    for cp in loads[:3]:
        cp.start()
    barrier = pltpu.get_barrier_semaphore()

    def greet(k, _):
        pl.semaphore_signal(barrier, inc=1, device_id=peer(k), device_id_type=MESH)
        return 0

    lax.fori_loop(1, ndev, greet, 0)
    for cp in near:
        cp.start()
    for cp in loads[3:]:
        cp.start()

    sub8 = iota((8, LANES), 0)
    lane8 = iota((8, LANES), 1)
    sub32 = iota((K, LANES), 0)
    lane32 = iota((K, LANES), 1)
    lane1 = iota((1, LANES), 1)

    loads[1].wait()
    sub128 = iota((LANES, LANES), 0)
    for i in range(chunks):
        lo = perm[i : i + 1, :] & (LANES - 1)
        oh[:, i * LANES : (i + 1) * LANES] = jnp.where(sub128 == lo, 1.0, 0.0).astype(BF16)
    loads[0].wait()
    for i in range(chunks):
        x32[i : i + 1, :] = kry[J - 1 : J, i * LANES : (i + 1) * LANES]
    x3 = jnp.concatenate(split3(x32[...]), axis=0)
    for i in range(chunks):
        a = jnp.dot(x3, oh[:, i * LANES : (i + 1) * LANES], preferred_element_type=F32)
        a = a[:chunks] + a[chunks : 2 * chunks] + a[2 * chunks :]
        hi = perm[i : i + 1, :] >> 7
        half = (i % 2) * LANES
        xown[i // 2 : i // 2 + 1, half : half + LANES] = rowsum(jnp.where(iota((chunks, LANES), 0) == hi, a, 0.0))

    loads[2].wait()
    loads[3].wait()
    tile = jnp.zeros((8, LANES), F32)
    qacc = jnp.zeros((K, LANES), F32)
    for t in range(groups):
        acc = jnp.zeros((K, LANES), F32)
        for cc in range(4):
            c = 4 * t + cc
            p = (
                basis[:, c * M : c * M + LANES] * xown[c : c + 1, :LANES]
                + basis[:, c * M + LANES : (c + 1) * M] * xown[c : c + 1, LANES:]
            )
            acc = acc + jnp.where(lane32 == cc * K + sub32, lanesum(p), 0.0)
        row = rowsum(acc)
        qacc = qacc + trans[:, t * LANES : (t + 1) * LANES] * row
        tile = jnp.where(sub8 == t, row, tile)
    qrow = rowsum(jnp.where((lane32 & (K - 1)) == sub32, lanesum(qacc), 0.0))
    land1[me] = jnp.where(sub8 == groups, qrow, tile)

    for cp in loads[6:]:
        cp.wait()
    gram = jnp.zeros((8, LANES), F32)
    for k in range(J):
        acc = jnp.zeros((8, LANES), F32)
        for i in range(chunks):
            part = kry[:, i * LANES : (i + 1) * LANES]
            acc = acc + part * kry[k : k + 1, i * LANES : (i + 1) * LANES]
        gram = gram + jnp.where((lane8 & (J - 1)) == k, lanesum(acc), 0.0)
    message = jnp.where((lane8 >> 3) == sub8, gram, 0.0)

    stride = ndev * 8
    for i in range(leaves * NF):
        s = owner_s[fsrc_s[i]]
        turn = (i % NF - s) & 3
        idx[i] = turn * stride + (s >> shift) * 8 + ((s & (leaves - 1)) >> 2)

    pl.semaphore_wait(barrier, ndev - 1)

    xbufs = (xown, xin1, xin2, xin3)
    xcopies = [
        pltpu.make_async_remote_copy(
            src_ref=xown,
            dst_ref=xbufs[g],
            send_sem=xsend.at[g],
            recv_sem=xrecv.at[g],
            device_id=peer(hop % ndev),
            device_id_type=MESH,
        )
        for g, hop in ((1, 1), (2, -1), (3, 2))
    ]
    for cp in xcopies:
        cp.start()

    def send1(k):
        return pltpu.make_async_remote_copy(
            src_ref=land1.at[me],
            dst_ref=land1.at[me],
            send_sem=s1.at[k],
            recv_sem=r1.at[k],
            device_id=peer(k),
            device_id_type=MESH,
        )

    def recv1(k):
        src = wrap(me - k + ndev)
        return pltpu.make_async_remote_copy(
            src_ref=land1.at[src],
            dst_ref=land1.at[src],
            send_sem=s1.at[k],
            recv_sem=r1.at[k],
            device_id=peer(k),
            device_id_type=MESH,
        )

    def start1(k, _):
        send1(k).start()
        return 0

    lax.fori_loop(1, ndev, start1, 0)

    rows = iota((leaves, M), 0)
    sub16 = iota((16, M), 0)
    yc = jnp.zeros((leaves, M), F32)
    for g in range(4):
        near[g].wait()
        if g:
            xcopies[g - 1].wait_recv()

        def slot(i, yc):
            n = g * CAP + i
            src = nsrc_s[n]
            loc = owner_s[jnp.maximum(src, 0)] & (leaves - 1)
            x = xbufs[g][pl.ds(loc, 1), :]
            xh = x.astype(BF16).astype(F32)
            lhs = jnp.where(sub16 == 0, xh, jnp.where(sub16 == 1, x - xh, 0.0)).astype(BF16)
            blk = nb[n]
            bh = blk.astype(BF16)
            bl = (blk - bh.astype(F32)).astype(BF16)
            dims = (((1,), (1,)), ((), ()))
            r = lax.dot_general(lhs, bh, dims, preferred_element_type=F32)
            r = r + lax.dot_general(lhs, bl, dims, preferred_element_type=F32)
            tgt = jnp.where(src >= 0, ntgt_s[n], -1)
            return yc + jnp.where(rows == tgt, r[0:1] + r[1:2], 0.0)

        yc = lax.fori_loop(0, CAP, slot, yc, unroll=True)

    def wait1(k, _):
        recv1(k).wait_recv()
        return 0

    lax.fori_loop(1, ndev, wait1, 0)

    got = land1[...].reshape(stride, LANES)
    rolled[0:stride, :] = got
    for s in range(1, 4):
        rolled[s * stride : (s + 1) * stride, :] = pltpu.roll(got, K * s, 1)
    loads[4].wait()
    loads[5].wait()
    gacc = jnp.zeros((K, LANES), F32)
    for t in range(ndev // 4):
        row = jnp.zeros((1, LANES), F32)
        for ee in range(4):
            e = 4 * t + ee
            row = row + jnp.where(((lane1 >> 5) == ee) & (me != e), land1[e, groups : groups + 1, :], 0.0)
        gacc = gacc + top[:, t * LANES : (t + 1) * LANES] * row
    gcol = lanesum(gacc)

    y3 = jnp.zeros((2 * chunks, LANES), F32)
    for c in range(leaves):
        t, cc = c // 4, c % 4
        if cc == 0:
            grow = rowsum(trans[:, t * LANES : (t + 1) * LANES] * gcol)
        r = jnp.zeros((1, LANES), F32)
        for f in range(NF):
            r = jnp.where((lane1 >> 5) == f, rolled[pl.ds(idx[c * NF + f], 1), :], r)
        acc = far[:, c * LANES : (c + 1) * LANES] * r + jnp.where(lane32 == cc * K + sub32, grow, 0.0)
        g = lanesum(acc)
        yrow = yc[c : c + 1, :] + rowsum(basis[:, c * M : (c + 1) * M] * g)
        hi = jnp.concatenate([perm[2 * c : 2 * c + 1, :], perm[2 * c + 1 : 2 * c + 2, :]], axis=1) >> 7
        hit = iota((chunks, M), 0) == hi
        top_half = yrow.astype(BF16).astype(F32)
        lhs = jnp.concatenate([jnp.where(hit, v, 0.0).astype(BF16) for v in (top_half, yrow - top_half)], axis=0)
        y3 = y3 + lax.dot_general(
            lhs, oh[:, c * M : (c + 1) * M], (((1,), (1,)), ((), ())), preferred_element_type=F32
        )
    y = y3[:chunks] + y3[chunks:]
    ybuf[...] = y

    acc = jnp.zeros((8, LANES), F32)
    sq = jnp.zeros((8, LANES), F32)
    for i in range(chunks):
        acc = acc + kry[:, i * LANES : (i + 1) * LANES] * ybuf[i : i + 1, :]
    for i in range(chunks // 8):
        sq = sq + ybuf[8 * i : 8 * i + 8, :] * ybuf[8 * i : 8 * i + 8, :]
    message = message + jnp.where(lane8 == 64 + sub8, lanesum(acc), 0.0)
    message = message + jnp.where(lane8 == 72, lanesum(sq), 0.0)
    land2[me] = rowsum(message)

    def send2(k):
        return pltpu.make_async_remote_copy(
            src_ref=land2.at[me],
            dst_ref=land2.at[me],
            send_sem=s2.at[k],
            recv_sem=r2.at[k],
            device_id=peer(k),
            device_id_type=MESH,
        )

    def recv2(k):
        src = wrap(me - k + ndev)
        return pltpu.make_async_remote_copy(
            src_ref=land2.at[src],
            dst_ref=land2.at[src],
            send_sem=s2.at[k],
            recv_sem=r2.at[k],
            device_id=peer(k),
            device_id_type=MESH,
        )

    def start2(k, _):
        send2(k).start()
        return 0

    def wait2(k, _):
        recv2(k).wait_recv()
        return 0

    lax.fori_loop(1, ndev, start2, 0)
    for cp in xcopies:
        cp.wait_send()

    def sent1(k, _):
        send1(k).wait_send()
        return 0

    lax.fori_loop(1, ndev, sent1, 0)
    lax.fori_loop(1, ndev, wait2, 0)

    sums = land2[0]
    for e in range(1, ndev):
        sums = sums + land2[e]
    ky = lanesum(jnp.where(lane8 == 64 + sub8, sums, 0.0))
    kx = lanesum(jnp.where(lane8 == (J - 1) * J + sub8, sums, 0.0))
    h = (0.5 * kx + ky) * (1.0 / total)
    is_x = iota((8, 1), 0) == J - 1
    d = h - jnp.where(is_x, 0.5, 0.0)
    left = rowsum(jnp.where((lane8 >> 3) == sub8, d, 0.0))
    right = rowsum(jnp.where((lane8 & (J - 1)) == sub8, d, 0.0))
    along = rowsum(jnp.where(lane8 == 64 + sub8, -2.0 * d, 0.0))
    terms = sums * (left * right + along + jnp.where(lane1 == 72, 1.0, 0.0))
    squares = jnp.maximum(lanesum(terms), 0.0) * (1.0 / total)
    beta = jnp.sqrt(squares + 1e-06)
    coef = rowsum(jnp.where(lane8 == sub8, h, 0.0)) + jnp.where(lane1 == J, beta, 0.0)
    out_ref[chunks:, :] = jnp.where(sub8 == 0, coef, 0.0)
    for i in range(chunks):
        out_ref[i : i + 1, :] = (ybuf[i : i + 1, :] - rowsum(kry[:, i * LANES : (i + 1) * LANES] * d)) / beta

    def sent2(k, _):
        send2(k).wait_send()
        return 0

    lax.fori_loop(1, ndev, sent2, 0)


def take_apart(both_ref, nxt_ref, coef_ref):
    nxt_ref[...] = both_ref[: nxt_ref.shape[0], :]
    coef_ref[...] = both_ref[nxt_ref.shape[0] : nxt_ref.shape[0] + 1, : J + 1]


def on_device(
    krylov,
    tree_perm,
    owner,
    near_src,
    near_tgt,
    near_blocks,
    basis,
    transfer,
    top_coup,
    far_src,
    far_coup,
):
    ndev = lax.axis_size("leaf")
    local_rows = tree_perm.shape[0]
    leaves = local_rows // M
    chunks = local_rows // LANES
    hbm = pl.BlockSpec(memory_space=pltpu.HBM)
    vmem = pl.BlockSpec(memory_space=pltpu.VMEM)
    arrays = (krylov, tree_perm.reshape(chunks, LANES), basis, transfer, top_coup, far_coup, near_blocks)
    indices = (owner, near_src, near_tgt, far_src)
    dma = pltpu.SemaphoreType.DMA
    both = pl.pallas_call(
        functools.partial(kernel, ndev, leaves, float(local_rows * ndev)),
        out_shape=jax.ShapeDtypeStruct((chunks + 8, LANES), F32),
        in_specs=[hbm] * 11,
        out_specs=vmem,
        scratch_shapes=[pltpu.VMEM(a.shape, a.dtype) for a in arrays]
        + [pltpu.SMEM(a.shape, a.dtype) for a in indices]
        + [
            pltpu.VMEM((chunks, LANES), F32),
            pltpu.VMEM((LANES, local_rows), BF16),
            pltpu.VMEM((leaves, M), F32),
            pltpu.VMEM((leaves, M), F32),
            pltpu.VMEM((leaves, M), F32),
            pltpu.VMEM((leaves, M), F32),
            pltpu.VMEM((ndev, 8, LANES), F32),
            pltpu.VMEM((ndev, 1, LANES), F32),
            pltpu.VMEM((4 * ndev * 8, LANES), F32),
            pltpu.SMEM((leaves * NF,), jnp.int32),
            pltpu.VMEM((chunks, LANES), F32),
            dma((10,)),
            dma((4,)),
            dma((4,)),
            dma((4,)),
            dma((ndev,)),
            dma((ndev,)),
            dma((ndev,)),
            dma((ndev,)),
        ],
        compiler_params=pltpu.CompilerParams(
            collective_id=0, has_side_effects=True, vmem_limit_bytes=60 * 1024 * 1024
        ),
        cost_estimate=pl.CostEstimate(flops=20_000_000, bytes_accessed=10_000_000, transcendentals=0),
    )(*arrays, *indices)
    nxt, coeffs = pl.pallas_call(
        take_apart,
        out_shape=(
            jax.ShapeDtypeStruct((chunks, LANES), F32),
            jax.ShapeDtypeStruct((1, J + 1), F32),
        ),
        in_specs=[vmem],
        out_specs=(vmem, vmem),
    )(both)
    return nxt.reshape(local_rows), coeffs.reshape(J + 1)


def solution(mesh):
    return jax.shard_map(
        on_device,
        mesh=mesh,
        in_specs=(
            P(None, ("parts", "leaf")),
            P(("parts", "leaf")),
            P("parts"),
            P(("parts", "leaf")),
            P(("parts", "leaf")),
            P(("parts", "leaf"), None, None),
            P(None, ("parts", "leaf")),
            P(None, ("parts", "leaf")),
            P(("parts", "leaf"), None),
            P(("parts", "leaf")),
            P(None, ("parts", "leaf")),
        ),
        out_specs=(P(("parts", "leaf")), P("parts")),
        check_vma=False,
    )
```
